32 devices in a mesh: section: 2 (over core), dp: 4 (over z), mp: 4 (over y, x).
Axes of the slice: x: 2, y: 2, z: 4, core: 2. Of those that a mesh axis runs over, the one named last changes fastest.
Arguments:
- features: bfloat16 [4096, 4096], P(('section', 'dp'), 'mp'), may hold values from -6 to 6
- w_in: bfloat16 [4096, 2048], P(('section', 'dp'), 'mp'), may hold values from -0.09375 to 0.09375
- w_out: bfloat16 [512, 2048], P(('section', 'dp'), 'mp'), may hold values from -0.125 to 0.125
- codebook: bfloat16 [3, 65536, 512], P(None, ('section', 'dp'), 'mp'), may hold values from -3 to 3
- codes: int32 [3, 4096], P(None, ('section', 'dp')), may hold values from 0 to 65535, as said below
- decoder_grad: bfloat16 [4096, 512], P(('section', 'dp'), 'mp'), may hold values from -6 to 6
Outputs:
- in_grad: float32 [4096, 2048], P(('section', 'dp'), 'mp')
- out_grad: float32 [512, 2048], P(('section', 'dp'), 'mp')
- code_sums: float32 [3, 65536, 512], P(None, ('section', 'dp'), 'mp')
The draws below stay inside these ranges and needn't reach their ends.
Inputs may be any that keep to these rules, and one draw needn't show every extreme that they name: Row k of a level's codebook belongs to owner k // 8192. Within the 512 items of one device (aligned blocks of items), at each level at most 128 codes belong to one owner; at each level some owner receives exactly 128 codes from every device's items.
All inputs are finite; a program needn't handle non-finite values.
Results may differ from the reference program's by a relative error of at most 0.0026.
Values may be sent and summed in bfloat16 or wider, within the bound.
A program may use at most 64 MiB of HBM per device.

```python
import jax
import jax.numpy as jnp
from jax import lax

D = 4096
H = 2048
L = 512
K = 65536
LEV = 3
ITEM_DEV = 512
OWNERS = 8
ITEMS = 4096
ROWS_OWN = 8192
CAP = 128


def draw_codes(key, part):
    levels = []
    for level_index in range(LEV):
        level_key = jax.random.fold_in(key, 17 + level_index)
        full_owner = jax.random.randint(jax.random.fold_in(level_key, 1), (), 0, OWNERS)
        block_keys = jax.random.split(jax.random.fold_in(level_key, 2), OWNERS)

        def one_block(block_key):
            pick_key, order_key, row_key = jax.random.split(block_key, 3)
            places = jax.random.permutation(pick_key, (OWNERS - 1) * CAP)[:ITEM_DEV - CAP]
            others = (places // CAP).astype(jnp.int32)
            others = others + (others >= full_owner).astype(jnp.int32)
            owners = jnp.concatenate([jnp.zeros((CAP,), jnp.int32) + full_owner, others])
            owners = jax.random.permutation(order_key, owners)
            offsets = jax.random.randint(row_key, (ITEM_DEV,), 0, ROWS_OWN)
            return owners * ROWS_OWN + offsets
        levels.append(jax.vmap(one_block)(block_keys).reshape(ITEMS))
    return jnp.stack(levels).astype(jnp.int32)


def strengthened(drawn, stream_key, source, target, blocks, factor):
    owner, partner = [(jnp.arange(drawn.shape[position]) // (drawn.shape[position] // blocks)).reshape([-1 if axis == position else 1 for axis in range(drawn.ndim)]) for position in (source, target)]
    chosen = jax.random.permutation(stream_key, blocks)[partner]
    strong = (owner == chosen) | (owner == (partner + blocks // 2) % blocks)
    return jnp.where(strong, factor * drawn, drawn)


def block_scale(own_key, shape, shards, smallest, largest):
    def one(axis_at, shards_of):
        draws = jax.random.uniform(jax.random.fold_in(jax.random.fold_in(own_key, 6), axis_at), (shards_of,), jnp.float32, smallest / len(shards), largest / len(shards))
        return jnp.repeat(jnp.exp(draws), shape[axis_at] // shards_of).reshape((-1,) + (1,) * (len(shape) - axis_at - 1))

    factor_of = one(*shards[0])
    for cut in shards[1:]:
        factor_of = factor_of * one(*cut)
    return factor_of


def centred(rng, extent, width, reach, cuts=(), held_as=jnp.bfloat16):
    result = width * jax.random.normal(rng, extent, jnp.float32)
    if cuts:
        result = result * block_scale(rng, extent, cuts, -0.22, 0.18)
    return jnp.clip(result, -reach, reach).astype(held_as)


def noise_with(rng, dims, spread, reach, cuts, heavy, kind=jnp.bfloat16):
    result = spread * jax.random.normal(rng, dims, jnp.float32)
    if cuts:
        result = result * block_scale(rng, dims, cuts, -0.22, 0.18)
    return jnp.clip(strengthened(result, jax.random.fold_in(rng, 3), *heavy), -reach, reach).astype(kind)


def setup_inputs(seed: int = 0) -> dict:
    keys = jax.random.split(jax.random.key(seed), 7)
    return {
        "features": noise_with(keys[0], (ITEMS, D), 1.0, 6.0, ((0, 8), (1, 4)), (0, 1, 8, 2.0)),
        "w_in": centred(keys[1], (D, H), D ** -0.5, 0.09375, ((0, 8), (1, 4))),
        "w_out": centred(keys[2], (L, H), H ** -0.5, 0.125, ((0, 8), (1, 4))),
        "codebook": centred(keys[3], (LEV, K, L), 0.5, 3.0, ((1, 8), (2, 4))),
        "codes": draw_codes(jax.random.fold_in(keys[6], 71), 0),
        "decoder_grad": noise_with(keys[5], (ITEMS, L), 1.0, 6.0, ((0, 8), (1, 4)), (0, 1, 8, 2.0)),
    }


BETA = 0.25

def silu_slope(preact):
    logistic = jax.nn.sigmoid(preact)
    return logistic * (1.0 + preact * (1.0 - logistic))

def reference(features, w_in, w_out, codebook, codes, decoder_grad):
    preact = jnp.dot(features, w_in, preferred_element_type=jnp.float32)
    hidden = jax.nn.silu(preact).astype(jnp.bfloat16)
    latent = lax.dot_general(hidden, w_out, (((1,), (1,)), ((), ())), preferred_element_type=jnp.float32)
    residual = latent
    pull_sum = jnp.zeros_like(latent)
    code_total = jnp.zeros((LEV * K, L), jnp.float32)
    for level_index in range(LEV):
        row_ids = codes[level_index].astype(jnp.int32)
        codeword = jnp.take(codebook[level_index], row_ids, axis=0).astype(jnp.float32)
        code_total = code_total.at[row_ids + level_index * K].add(residual)
        residual = residual - codeword
        pull_sum = pull_sum + residual
    latent_grad = ((decoder_grad.astype(jnp.float32) + 2.0 * BETA * pull_sum) / jnp.sqrt(jnp.float32(ITEMS))).astype(jnp.bfloat16)
    out_grad = lax.dot_general(latent_grad, hidden, (((0,), (0,)), ((), ())), preferred_element_type=jnp.float32)
    back_hidden = jnp.dot(latent_grad, w_out, preferred_element_type=jnp.float32)
    pre_grad = (back_hidden * silu_slope(preact)).astype(jnp.bfloat16)
    in_grad = lax.dot_general(features, pre_grad, (((0,), (0,)), ((), ())), preferred_element_type=jnp.float32)
    return (in_grad, out_grad, code_total.reshape(LEV, K, L))
```

```python
import functools

import jax
import jax.numpy as jnp
from jax import lax
from jax.experimental import pallas as pl
from jax.experimental.pallas import tpu as pltpu
from jax.sharding import PartitionSpec as P

BETA = 0.25
F32 = jnp.float32
BF16 = jnp.bfloat16


def partner_pairs(size, step):
    if size & (size - 1) == 0:
        return [(k, k ^ step) for k in range(size)]
    return [(k, (k + step) % size) for k in range(size)]


def source_of(me, size, step):
    if size & (size - 1) == 0:
        return me ^ step
    return (me + size - step) % size


def target_of(me, size, step):
    if size & (size - 1) == 0:
        return me ^ step
    return (me + step) % size


def shift(value, axis, step):
    return lax.ppermute(value, axis, partner_pairs(lax.axis_size(axis), step))


def sums_kernel(rows_ref, values_ref, out_ref):
    tile = out_ref.shape[1]
    slots = rows_ref.shape[2]
    first = pl.program_id(1) * tile
    row_ids = first + lax.broadcasted_iota(jnp.int32, (tile, slots), 0)
    chosen = jnp.where(row_ids == rows_ref[0], 1.0, 0.0).astype(BF16)
    out_ref[0] = jnp.dot(chosen, values_ref[0], preferred_element_type=F32)


def sum_rows(rows, values, rows_own):
    levels, slots = rows.shape
    width = values.shape[2]
    tile = min(512, rows_own)
    return pl.pallas_call(
        sums_kernel,
        grid=(levels, rows_own // tile),
        in_specs=[
            pl.BlockSpec((1, 1, slots), lambda level, part: (level, 0, 0)),
            pl.BlockSpec((1, slots, width), lambda level, part: (level, 0, 0)),
        ],
        out_specs=pl.BlockSpec((1, tile, width), lambda level, part: (level, part, 0)),
        out_shape=jax.ShapeDtypeStruct((levels, rows_own, width), F32),
        compiler_params=pltpu.CompilerParams(vmem_limit_bytes=24 * 2**20),
        cost_estimate=pl.CostEstimate(
            flops=2 * levels * rows_own * slots * width,
            bytes_accessed=4 * levels * rows_own * width,
            transcendentals=0,
        ),
    )(rows.reshape(levels, 1, slots), values)


def shards(features, w_in, w_out, codebook, codes, decoder_grad):
    n_sec, n_dp, n_mp = (lax.axis_size(a) for a in ("section", "dp", "mp"))
    sec, dp, mp = (lax.axis_index(a) for a in ("section", "dp", "mp"))
    owners = n_sec * n_dp
    me = sec * n_dp + dp
    items, in_part = features.shape
    in_rows, hid = w_in.shape
    out_rows = w_out.shape[0]
    levels, rows_own, width = codebook.shape
    capacity = max(2, 2 * items // owners)
    slots = owners * capacity
    items_all = items * owners

    w_parts = [(dp, w_in, w_out)]
    f_parts = [(mp, features)]
    for step in range(1, n_dp):
        w_parts.append((source_of(dp, n_dp, step), shift(w_in, "dp", step), shift(w_out, "dp", step)))
    for step in range(1, n_mp):
        f_parts.append((source_of(mp, n_mp, step), shift(features, "mp", step)))
    blocks = [(sec * n_dp + at, a, b) for at, a, b in w_parts]
    for step in range(1, n_sec):
        from_sec = source_of(sec, n_sec, step)
        blocks += [
            (from_sec * n_dp + at, shift(a, "section", step), shift(b, "section", step))
            for at, a, b in w_parts
        ]
    w_full = jnp.zeros((owners * in_rows, hid), BF16)
    out_full = jnp.zeros((owners * out_rows, hid), BF16)
    for at, a, b in blocks:
        w_full = lax.dynamic_update_slice(w_full, a, (at * in_rows, 0))
        out_full = lax.dynamic_update_slice(out_full, b, (at * out_rows, 0))
    f_full = jnp.zeros((items, n_mp * in_part), BF16)
    for at, a in f_parts:
        f_full = lax.dynamic_update_slice(f_full, a, (0, at * in_part))

    exchange = functools.partial(
        lax.all_to_all, axis_name=("section", "dp"), split_axis=0, concat_axis=0, tiled=True
    )
    all_codes = exchange(jnp.broadcast_to(codes[None], (owners, levels, items)))
    mine = all_codes // rows_own == me
    before = jnp.arange(items)[:, None] < jnp.arange(items)[None, :]
    place = jnp.dot(
        mine.reshape(-1, items).astype(BF16), before.astype(BF16), preferred_element_type=F32
    ).astype(jnp.int32).reshape(owners, levels, items)
    place = jnp.where(mine, place, capacity)
    local = all_codes % rows_own
    hit = place[:, :, None, :] == jnp.arange(capacity)[None, None, :, None]
    asked = jnp.sum(jnp.where(hit, local[:, :, None, :], 0), axis=3)
    book = codebook.reshape(levels * rows_own, width)
    flat_asked = asked + (jnp.arange(levels) * rows_own)[None, :, None]
    answers = exchange(jnp.take(book, flat_asked, axis=0, mode="clip"))
    owner_of = codes // rows_own
    same = (owner_of[:, :, None] == owner_of[:, None, :]) & before.T[None]
    ranking = jnp.sum(same.astype(jnp.int32), axis=2)
    level_ids = jnp.arange(levels, dtype=jnp.int32)[:, None]
    codewords = jnp.take(
        answers.reshape(owners * levels * capacity, width),
        (owner_of * levels + level_ids) * capacity + ranking,
        axis=0,
        mode="clip",
    )

    preact = jnp.dot(f_full, w_full, preferred_element_type=F32)
    hidden = jax.nn.silu(preact).astype(BF16)
    latent = None
    for step in list(range(1, n_mp)) + [0]:
        goes_to = target_of(mp, n_mp, step)
        rows = lax.dynamic_slice(out_full, (goes_to * width, 0), (width, hid))
        part = lax.dot_general(hidden, rows, (((1,), (1,)), ((), ())), preferred_element_type=F32)
        part = shift(part, "mp", step) if step else part
        latent = part if latent is None else latent + part

    residual = latent
    pull_sum = jnp.zeros_like(latent)
    inputs = []
    for level in range(levels):
        inputs.append(residual.astype(BF16))
        residual = residual - codewords[level].astype(F32)
        pull_sum = pull_sum + residual
    latent_grad = (
        (decoder_grad.astype(F32) + 2.0 * BETA * pull_sum) / jnp.sqrt(F32(items_all))
    ).astype(BF16)

    grad_full = jnp.zeros((items, n_mp * width), BF16)
    for step in range(n_mp):
        got = shift(latent_grad, "mp", step) if step else latent_grad
        at = source_of(mp, n_mp, step) if step else mp
        grad_full = lax.dynamic_update_slice(grad_full, got, (0, at * width))

    slot_of = owner_of * capacity + ranking
    pick = (jnp.arange(slots)[None, :, None] == slot_of[:, None, :]).astype(BF16)
    outgoing = lax.dot_general(
        pick, jnp.stack(inputs), (((2,), (1,)), ((0,), (0,))), preferred_element_type=F32
    ).astype(BF16)
    outgoing = outgoing.reshape(levels, owners, capacity, width).transpose(1, 0, 2, 3)
    incoming = exchange(outgoing)
    code_sums = sum_rows(
        asked.transpose(1, 0, 2).reshape(levels, slots),
        incoming.transpose(1, 0, 2, 3).reshape(levels, slots, width),
        rows_own,
    )

    back_hidden = jnp.dot(grad_full, out_full, preferred_element_type=F32)
    logistic = jax.nn.sigmoid(preact)
    slope = logistic * (1.0 + preact * (1.0 - logistic))
    pre_grad = (back_hidden * slope).astype(BF16)
    over_items = functools.partial(
        lax.dot_general, dimension_numbers=(((0,), (0,)), ((), ())), preferred_element_type=F32
    )

    def in_chunk(at):
        return over_items(lax.dynamic_slice(f_full, (0, at * in_rows), (items, in_rows)), pre_grad)

    def out_chunk(at):
        return over_items(lax.dynamic_slice(grad_full, (0, at * out_rows), (items, out_rows)), hidden)

    def scattered(chunk):
        total = None
        for step in list(range(n_dp - 1, 0, -1)) + [0]:
            goes_to = target_of(dp, n_dp, step) if step else dp
            pair = None
            for other in list(range(1, n_sec)) + [0]:
                to_sec = target_of(sec, n_sec, other) if other else sec
                part = chunk(to_sec * n_dp + goes_to)
                if other:
                    part = shift(part.astype(BF16), "section", other).astype(F32)
                pair = part if pair is None else pair + part
            if step:
                pair = shift(pair.astype(BF16), "dp", step).astype(F32)
            total = pair if total is None else total + pair
        return total

    out_grad = scattered(out_chunk)
    in_grad = scattered(in_chunk)
    return (in_grad, out_grad, code_sums)


def solution(mesh):
    owned = P(("section", "dp"), "mp")
    book = P(None, ("section", "dp"), "mp")
    return jax.shard_map(
        shards,
        mesh=mesh,
        in_specs=(owned, owned, owned, book, P(None, ("section", "dp")), owned),
        out_specs=(owned, owned, book),
        check_vma=False,
    )
```

```python
import functools

import jax
import jax.numpy as jnp
from jax import lax
from jax.experimental import pallas as pl
from jax.experimental.pallas import tpu as pltpu
from jax.sharding import PartitionSpec as P

BETA = 0.25
F32 = jnp.float32
BF16 = jnp.bfloat16


def partner_pairs(size, step):
    if size & (size - 1) == 0:
        return [(k, k ^ step) for k in range(size)]
    return [(k, (k + step) % size) for k in range(size)]


def source_of(me, size, step):
    if size & (size - 1) == 0:
        return me ^ step
    return (me + size - step) % size


def target_of(me, size, step):
    if size & (size - 1) == 0:
        return me ^ step
    return (me + step) % size


def shift(value, axis, step):
    return lax.ppermute(value, axis, partner_pairs(lax.axis_size(axis), step))


def sums_kernel(rows_ref, values_ref, out_ref):
    tile = out_ref.shape[1]
    slots = rows_ref.shape[2]
    first = pl.program_id(1) * tile
    row_ids = first + lax.broadcasted_iota(jnp.int32, (tile, slots), 0)
    chosen = jnp.where(row_ids == rows_ref[0], 1.0, 0.0).astype(BF16)
    out_ref[0] = jnp.dot(chosen, values_ref[0], preferred_element_type=F32)


def sum_rows(rows, values, rows_own):
    levels, slots = rows.shape
    width = values.shape[2]
    tile = min(512, rows_own)
    return pl.pallas_call(
        sums_kernel,
        grid=(levels, rows_own // tile),
        in_specs=[
            pl.BlockSpec((1, 1, slots), lambda level, part: (level, 0, 0)),
            pl.BlockSpec((1, slots, width), lambda level, part: (level, 0, 0)),
        ],
        out_specs=pl.BlockSpec((1, tile, width), lambda level, part: (level, part, 0)),
        out_shape=jax.ShapeDtypeStruct((levels, rows_own, width), F32),
        compiler_params=pltpu.CompilerParams(vmem_limit_bytes=24 * 2**20),
        cost_estimate=pl.CostEstimate(
            flops=2 * levels * rows_own * slots * width,
            bytes_accessed=4 * levels * rows_own * width,
            transcendentals=0,
        ),
    )(rows.reshape(levels, 1, slots), values)


def gather_kernel(
    f_ref, w_ref, o_ref, ans_ref, f_out, w_out, o_out, ans_out,
    local_sem, f_send, f_recv, dp_send, dp_recv, sec_send, sec_recv, ans_send, ans_recv,
):
    n_dp, n_mp = lax.axis_size("dp"), lax.axis_size("mp")
    sec, dp, mp = (lax.axis_index(a) for a in ("section", "dp", "mp"))
    owners = ans_ref.shape[0]
    me = sec * n_dp + dp
    base = sec * n_dp
    other = {"section": 1 - sec}
    items, in_part = f_ref.shape
    barrier = pltpu.get_barrier_semaphore()

    def owner_at(step):
        at = lax.rem(me + step, owners)
        return at, {"section": at // n_dp, "dp": lax.rem(at, n_dp)}

    for step in range(1, owners):
        pl.semaphore_signal(barrier, inc=1, device_id=owner_at(step)[1], device_id_type=pl.DeviceIdType.MESH)
    for step in range(1, n_mp):
        pl.semaphore_signal(
            barrier, inc=1, device_id={"mp": target_of(mp, n_mp, step)}, device_id_type=pl.DeviceIdType.MESH
        )
    pl.semaphore_wait(barrier, owners - 1 + n_mp - 1)

    def remote(src, dst, send, recv, to):
        return pltpu.make_async_remote_copy(
            src_ref=src, dst_ref=dst, send_sem=send, recv_sem=recv,
            device_id=to, device_id_type=pl.DeviceIdType.MESH,
        )

    def columns(at):
        return pl.ds(pl.multiple_of(at * in_part, in_part), in_part)

    answers = []
    for step in range(1, owners):
        at, to = owner_at(step)
        answers.append(remote(ans_ref.at[at], ans_out.at[me], ans_send.at[step], ans_recv.at[step], to))
        answers[-1].start()

    relay = n_mp == 4
    feature = [
        remote(
            f_ref, f_out.at[:, columns(mp)], f_send.at[step], f_recv.at[step],
            {"mp": target_of(mp, n_mp, step)},
        )
        for step in (range(1, 3) if relay else range(1, n_mp))
    ]

    def weights(block, src, side, step, to):
        sems = (dp_send, dp_recv) if side < 2 else (sec_send, sec_recv)
        place = side if side < 2 else side - 2
        pairs = ((w_ref, w_out), (o_ref, o_out))
        return [
            remote(
                own if src is None else out.at[src], out.at[block],
                sems[0].at[place, step, k], sems[1].at[place, step, k], to,
            )
            for k, (own, out) in enumerate(pairs)
        ]

    def start(copies):
        for copy in copies:
            copy.start()

    right, left = {"dp": dp + 1}, {"dp": dp - 1}

    @pl.when(dp < n_dp - 1)
    def _():
        start(weights(me, None, 0, 0, right))

    @pl.when(dp > 0)
    def _():
        start(weights(me, None, 1, 0, left))

    start(feature)
    own_sec = weights(me, None, 2, n_dp - 1, other)
    start(own_sec)
    locals_ = [
        pltpu.make_async_copy(f_ref, f_out.at[:, columns(mp)], local_sem.at[0]),
        pltpu.make_async_copy(w_ref, w_out.at[me], local_sem.at[1]),
        pltpu.make_async_copy(o_ref, o_out.at[me], local_sem.at[2]),
        pltpu.make_async_copy(ans_ref.at[me], ans_out.at[me], local_sem.at[3]),
    ]
    start(locals_)

    def arrive(block, side, step):
        for copy in weights(block, block, side, step, other):
            copy.wait_recv()

    halves = []
    for step in range(n_dp - 1):
        @pl.when(dp - 1 - step >= 0)
        def _(step=step):
            block = base + dp - 1 - step
            arrive(block, 0, step)
            if step + 1 < n_dp - 1:
                @pl.when(dp < n_dp - 1)
                def _():
                    start(weights(block, block, 0, step + 1, right))
            start(weights(block, block, 2, step, other))

        @pl.when(dp + 1 + step <= n_dp - 1)
        def _(step=step):
            block = base + dp + 1 + step
            arrive(block, 1, step)
            if step + 1 < n_dp - 1:
                @pl.when(dp > 0)
                def _():
                    start(weights(block, block, 1, step + 1, left))
            start(weights(block, block, 3, step, other))

        if step == 0:
            for copy in feature:
                copy.wait_recv()
            if relay:
                half = items // 2
                for k, (source, to) in enumerate(((mp ^ 1, mp ^ 2), (mp ^ 2, mp ^ 1))):
                    view = f_out.at[pl.ds(k * half, half), columns(source)]
                    halves.append(remote(view, view, f_send.at[3 + k], f_recv.at[3 + k], {"mp": to}))
                start(halves)

    for copy in locals_ + answers:
        copy.wait()
    for copy in feature:
        copy.wait_send()
    if relay:
        for k in range(2):
            view = f_out.at[pl.ds(k * (items // 2), items // 2), columns(mp ^ 3)]
            remote(view, view, f_send.at[3 + k], f_recv.at[3 + k], {"mp": mp ^ 1}).wait_recv()
            halves[k].wait_send()
    elsewhere = (1 - sec) * n_dp
    for copy in own_sec:
        copy.wait_send()
    arrive(elsewhere + dp, 2, n_dp - 1)

    def sent(block, side, step):
        for copy in weights(block, block, side, step, other):
            copy.wait_send()

    @pl.when(dp < n_dp - 1)
    def _():
        sent(me, 0, 0)

    @pl.when(dp > 0)
    def _():
        sent(me, 1, 0)

    for step in range(n_dp - 1):
        @pl.when(dp - 1 - step >= 0)
        def _(step=step):
            if step + 1 < n_dp - 1:
                @pl.when(dp < n_dp - 1)
                def _():
                    sent(me, 0, step + 1)
            sent(me, 2, step)
            arrive(elsewhere + dp - 1 - step, 2, step)

        @pl.when(dp + 1 + step <= n_dp - 1)
        def _(step=step):
            if step + 1 < n_dp - 1:
                @pl.when(dp > 0)
                def _():
                    sent(me, 1, step + 1)
            sent(me, 3, step)
            arrive(elsewhere + dp + 1 + step, 3, step)


def gather_all(features, w_in, w_out, answers):
    n_dp, n_mp = lax.axis_size("dp"), lax.axis_size("mp")
    owners = answers.shape[0]
    items, in_part = features.shape
    dma = pltpu.SemaphoreType.DMA
    anywhere = pl.BlockSpec(memory_space=pl.ANY)
    return pl.pallas_call(
        gather_kernel,
        out_shape=(
            jax.ShapeDtypeStruct((items, n_mp * in_part), BF16),
            jax.ShapeDtypeStruct((owners, *w_in.shape), BF16),
            jax.ShapeDtypeStruct((owners, *w_out.shape), BF16),
            jax.ShapeDtypeStruct(answers.shape, BF16),
        ),
        in_specs=[anywhere] * 4,
        out_specs=[anywhere] * 4,
        scratch_shapes=[
            dma((4,)), dma((n_mp + 1,)), dma((n_mp + 1,)),
            dma((2, n_dp, 2)), dma((2, n_dp, 2)), dma((2, n_dp, 2)), dma((2, n_dp, 2)),
            dma((owners,)), dma((owners,)),
        ],
        compiler_params=pltpu.CompilerParams(collective_id=0, has_side_effects=True),
    )(features, w_in, w_out, answers)


def shards(features, w_in, w_out, codebook, codes, decoder_grad):
    n_sec, n_dp, n_mp = (lax.axis_size(a) for a in ("section", "dp", "mp"))
    sec, dp, mp = (lax.axis_index(a) for a in ("section", "dp", "mp"))
    owners = n_sec * n_dp
    me = sec * n_dp + dp
    items, in_part = features.shape
    in_rows, hid = w_in.shape
    out_rows = w_out.shape[0]
    levels, rows_own, width = codebook.shape
    capacity = max(2, 2 * items // owners)
    slots = owners * capacity
    items_all = items * owners

    exchange = functools.partial(
        lax.all_to_all, axis_name=("section", "dp"), split_axis=0, concat_axis=0, tiled=True
    )
    all_codes = exchange(jnp.broadcast_to(codes[None], (owners, levels, items)))
    mine = all_codes // rows_own == me
    before = jnp.arange(items)[:, None] < jnp.arange(items)[None, :]
    place = jnp.dot(
        mine.reshape(-1, items).astype(BF16), before.astype(BF16), preferred_element_type=F32
    ).astype(jnp.int32).reshape(owners, levels, items)
    place = jnp.where(mine, place, capacity)
    local = all_codes % rows_own
    hit = place[:, :, None, :] == jnp.arange(capacity)[None, None, :, None]
    asked = jnp.sum(jnp.where(hit, local[:, :, None, :], 0), axis=3)
    book = codebook.reshape(levels * rows_own, width)
    flat_asked = asked + (jnp.arange(levels) * rows_own)[None, :, None]
    f_full, w_full, out_full, answers = gather_all(
        features, w_in, w_out, jnp.take(book, flat_asked, axis=0, mode="clip")
    )
    w_full = w_full.reshape(owners * in_rows, hid)
    out_full = out_full.reshape(owners * out_rows, hid)
    owner_of = codes // rows_own
    same = (owner_of[:, :, None] == owner_of[:, None, :]) & before.T[None]
    ranking = jnp.sum(same.astype(jnp.int32), axis=2)
    level_ids = jnp.arange(levels, dtype=jnp.int32)[:, None]
    codewords = jnp.take(
        answers.reshape(owners * levels * capacity, width),
        (owner_of * levels + level_ids) * capacity + ranking,
        axis=0,
        mode="clip",
    )

    preact = jnp.dot(f_full, w_full, preferred_element_type=F32)
    hidden = jax.nn.silu(preact).astype(BF16)
    latent = None
    for step in list(range(1, n_mp)) + [0]:
        goes_to = target_of(mp, n_mp, step)
        rows = lax.dynamic_slice(out_full, (goes_to * width, 0), (width, hid))
        part = lax.dot_general(hidden, rows, (((1,), (1,)), ((), ())), preferred_element_type=F32)
        part = shift(part, "mp", step) if step else part
        latent = part if latent is None else latent + part

    residual = latent
    pull_sum = jnp.zeros_like(latent)
    inputs = []
    for level in range(levels):
        inputs.append(residual.astype(BF16))
        residual = residual - codewords[level].astype(F32)
        pull_sum = pull_sum + residual
    latent_grad = (
        (decoder_grad.astype(F32) + 2.0 * BETA * pull_sum) / jnp.sqrt(F32(items_all))
    ).astype(BF16)

    grad_full = jnp.zeros((items, n_mp * width), BF16)
    for step in range(n_mp):
        got = shift(latent_grad, "mp", step) if step else latent_grad
        at = source_of(mp, n_mp, step) if step else mp
        grad_full = lax.dynamic_update_slice(grad_full, got, (0, at * width))

    slot_of = owner_of * capacity + ranking
    pick = (jnp.arange(slots)[None, :, None] == slot_of[:, None, :]).astype(BF16)
    outgoing = lax.dot_general(
        pick, jnp.stack(inputs), (((2,), (1,)), ((0,), (0,))), preferred_element_type=F32
    ).astype(BF16)
    outgoing = outgoing.reshape(levels, owners, capacity, width).transpose(1, 0, 2, 3)
    incoming = exchange(outgoing)
    code_sums = sum_rows(
        asked.transpose(1, 0, 2).reshape(levels, slots),
        incoming.transpose(1, 0, 2, 3).reshape(levels, slots, width),
        rows_own,
    )

    back_hidden = jnp.dot(grad_full, out_full, preferred_element_type=F32)
    logistic = jax.nn.sigmoid(preact)
    slope = logistic * (1.0 + preact * (1.0 - logistic))
    pre_grad = (back_hidden * slope).astype(BF16)
    over_items = functools.partial(
        lax.dot_general, dimension_numbers=(((0,), (0,)), ((), ())), preferred_element_type=F32
    )

    def in_chunk(at):
        return over_items(lax.dynamic_slice(f_full, (0, at * in_rows), (items, in_rows)), pre_grad)

    def out_chunk(at):
        return over_items(lax.dynamic_slice(grad_full, (0, at * out_rows), (items, out_rows)), hidden)

    def scattered(chunk, sums):
        parts = []
        for step in list(range(n_dp - 1, 0, -1)) + [0]:
            goes_to = target_of(dp, n_dp, step) if step else dp
            pair = None
            for other in list(range(1, n_sec)) + [0]:
                to_sec = target_of(sec, n_sec, other) if other else sec
                part = chunk(to_sec * n_dp + goes_to)
                if other:
                    part = shift(part.astype(BF16), "section", other).astype(F32)
                pair = part if pair is None else pair + part
            if step:
                pair = shift(pair.astype(BF16), "dp", step).astype(F32)
            elif sums is not None:
                pair, sums = lax.optimization_barrier((pair, sums))
            parts.append(pair)
        total = parts[-1]
        for pair in parts[:-1]:
            total = total + pair
        return total, sums

    out_grad, _ = scattered(out_chunk, None)
    in_grad, code_sums = scattered(in_chunk, code_sums)
    return (in_grad, out_grad, code_sums)


def solution(mesh):
    owned = P(("section", "dp"), "mp")
    book = P(None, ("section", "dp"), "mp")
    return jax.shard_map(
        shards,
        mesh=mesh,
        in_specs=(owned, owned, owned, book, P(None, ("section", "dp")), owned),
        out_specs=(owned, owned, book),
        check_vma=False,
    )
```

```python
import functools

import jax
import jax.numpy as jnp
from jax import lax
from jax.experimental import pallas as pl
from jax.experimental.pallas import tpu as pltpu
from jax.sharding import PartitionSpec as P

BETA = 0.25
F32 = jnp.float32
BF16 = jnp.bfloat16


def partner_pairs(size, step):
    if size & (size - 1) == 0:
        return [(k, k ^ step) for k in range(size)]
    return [(k, (k + step) % size) for k in range(size)]


def source_of(me, size, step):
    if size & (size - 1) == 0:
        return me ^ step
    return (me + size - step) % size


def target_of(me, size, step):
    if size & (size - 1) == 0:
        return me ^ step
    return (me + step) % size


def shift(value, axis, step):
    return lax.ppermute(value, axis, partner_pairs(lax.axis_size(axis), step))


def sums_kernel(rows_ref, values_ref, out_ref):
    tile = out_ref.shape[1]
    slots = rows_ref.shape[2]
    first = pl.program_id(1) * tile
    row_ids = first + lax.broadcasted_iota(jnp.int32, (tile, slots), 0)
    chosen = jnp.where(row_ids == rows_ref[0], 1.0, 0.0).astype(BF16)
    out_ref[0] = jnp.dot(chosen, values_ref[0], preferred_element_type=F32)


def sum_rows(rows, values, rows_own):
    levels, slots = rows.shape
    width = values.shape[2]
    tile = min(512, rows_own)
    return pl.pallas_call(
        sums_kernel,
        grid=(levels, rows_own // tile),
        in_specs=[
            pl.BlockSpec((1, 1, slots), lambda level, part: (level, 0, 0)),
            pl.BlockSpec((1, slots, width), lambda level, part: (level, 0, 0)),
        ],
        out_specs=pl.BlockSpec((1, tile, width), lambda level, part: (level, part, 0)),
        out_shape=jax.ShapeDtypeStruct((levels, rows_own, width), F32),
        compiler_params=pltpu.CompilerParams(vmem_limit_bytes=24 * 2**20),
        cost_estimate=pl.CostEstimate(
            flops=2 * levels * rows_own * slots * width,
            bytes_accessed=4 * levels * rows_own * width,
            transcendentals=0,
        ),
    )(rows.reshape(levels, 1, slots), values)


def gather_kernel(
    f_ref, fx_ref, fy_ref, w_ref, r1_ref, r2_ref, l1_ref, l2_ref, o_ref, ans_ref,
    f_out, w_out, o_out, ans_out, local_sem, early_sem, f_send, f_recv, dp_send, dp_recv, sec_send, sec_recv, ans_send, ans_recv,
):
    n_dp, n_mp = lax.axis_size("dp"), lax.axis_size("mp")
    sec, dp, mp = (lax.axis_index(a) for a in ("section", "dp", "mp"))
    owners = ans_ref.shape[0]
    me = sec * n_dp + dp
    base = sec * n_dp
    other = {"section": 1 - sec}
    items, in_part = f_ref.shape
    barrier = pltpu.get_barrier_semaphore()

    def owner_at(step):
        at = lax.rem(me + step, owners)
        return at, {"section": at // n_dp, "dp": lax.rem(at, n_dp)}

    for step in range(1, owners):
        pl.semaphore_signal(barrier, inc=1, device_id=owner_at(step)[1], device_id_type=pl.DeviceIdType.MESH)
    for step in range(1, n_mp):
        pl.semaphore_signal(
            barrier, inc=1, device_id={"mp": target_of(mp, n_mp, step)}, device_id_type=pl.DeviceIdType.MESH
        )
    pl.semaphore_wait(barrier, owners - 1 + n_mp - 1)

    def remote(src, dst, send, recv, to):
        return pltpu.make_async_remote_copy(
            src_ref=src, dst_ref=dst, send_sem=send, recv_sem=recv,
            device_id=to, device_id_type=pl.DeviceIdType.MESH,
        )

    def columns(at):
        return pl.ds(pl.multiple_of(at * in_part, in_part), in_part)

    answers = []
    for step in range(1, owners):
        at, to = owner_at(step)
        answers.append(remote(ans_ref.at[at], ans_out.at[me], ans_send.at[step], ans_recv.at[step], to))
        answers[-1].start()

    half = items // 2
    early = ((r1_ref, r2_ref), (l1_ref, l2_ref))
    halves = []
    for k, (ref, to) in enumerate(((fx_ref, mp ^ 2), (fy_ref, mp ^ 1))):
        rows = pl.ds(k * half, half)
        halves.append(
            remote(
                ref.at[rows], f_out.at[rows, columns(to ^ 3)], f_send.at[k], f_recv.at[k], {"mp": to}
            )
        )

    def weights(block, src, side, step, to):
        along = side < 2
        place = side if along else side - 2
        sems = (dp_send, dp_recv) if along else (sec_send, sec_recv)
        came = step - 1 if along else step
        copies = []
        for k, (own, out) in enumerate(((w_ref, w_out), (o_ref, o_out))):
            if k == 0 and along and step < 2:
                continue
            held = early[place][came] if k == 0 and 0 <= came < 2 else out.at[block]
            copies.append(
                remote(
                    own if src is None else held, out.at[block],
                    sems[0].at[place, step, k], sems[1].at[place, step, k], to,
                )
            )
        return copies

    def early_copy(block, side, step):
        return pltpu.make_async_copy(early[side][step], w_out.at[block], early_sem.at[side, step])

    def start(copies):
        for copy in copies:
            copy.start()

    right, left = {"dp": dp + 1}, {"dp": dp - 1}

    @pl.when(dp < n_dp - 1)
    def _():
        start(weights(me, None, 0, 0, right))

    @pl.when(dp > 0)
    def _():
        start(weights(me, None, 1, 0, left))

    start(halves)
    own_sec = weights(me, None, 2, n_dp - 1, other)
    start(own_sec)
    locals_ = [
        pltpu.make_async_copy(f_ref, f_out.at[:, columns(mp)], local_sem.at[0]),
        pltpu.make_async_copy(fx_ref, f_out.at[:, columns(mp ^ 1)], local_sem.at[4]),
        pltpu.make_async_copy(fy_ref, f_out.at[:, columns(mp ^ 2)], local_sem.at[5]),
        pltpu.make_async_copy(w_ref, w_out.at[me], local_sem.at[1]),
        pltpu.make_async_copy(o_ref, o_out.at[me], local_sem.at[2]),
        pltpu.make_async_copy(ans_ref.at[me], ans_out.at[me], local_sem.at[3]),
    ]
    start(locals_)

    def arrive(block, side, step):
        for copy in weights(block, block, side, step, other):
            copy.wait_recv()

    for step in range(n_dp - 1):
        @pl.when(dp - 1 - step >= 0)
        def _(step=step):
            block = base + dp - 1 - step
            if step < 2:
                early_copy(block, 0, step).start()
            arrive(block, 0, step)
            if step + 1 < n_dp - 1:
                @pl.when(dp < n_dp - 1)
                def _():
                    start(weights(block, block, 0, step + 1, right))
            start(weights(block, block, 2, step, other))

        @pl.when(dp + 1 + step <= n_dp - 1)
        def _(step=step):
            block = base + dp + 1 + step
            if step < 2:
                early_copy(block, 1, step).start()
            arrive(block, 1, step)
            if step + 1 < n_dp - 1:
                @pl.when(dp > 0)
                def _():
                    start(weights(block, block, 1, step + 1, left))
            start(weights(block, block, 3, step, other))

    for copy in locals_ + answers:
        copy.wait()
    for copy in halves:
        copy.wait_send()
    for k in range(2):
        view = f_out.at[pl.ds(k * half, half), columns(mp ^ 3)]
        remote(view, view, f_send.at[k], f_recv.at[k], {"mp": mp ^ 1}).wait_recv()
    elsewhere = (1 - sec) * n_dp
    for copy in own_sec:
        copy.wait_send()
    arrive(elsewhere + dp, 2, n_dp - 1)

    def sent(block, side, step):
        for copy in weights(block, block, side, step, other):
            copy.wait_send()

    @pl.when(dp < n_dp - 1)
    def _():
        sent(me, 0, 0)

    @pl.when(dp > 0)
    def _():
        sent(me, 1, 0)

    for step in range(n_dp - 1):
        @pl.when(dp - 1 - step >= 0)
        def _(step=step):
            if step + 1 < n_dp - 1:
                @pl.when(dp < n_dp - 1)
                def _():
                    sent(me, 0, step + 1)
            if step < 2:
                early_copy(base + dp - 1 - step, 0, step).wait()
            sent(me, 2, step)
            arrive(elsewhere + dp - 1 - step, 2, step)

        @pl.when(dp + 1 + step <= n_dp - 1)
        def _(step=step):
            if step + 1 < n_dp - 1:
                @pl.when(dp > 0)
                def _():
                    sent(me, 1, step + 1)
            if step < 2:
                early_copy(base + dp + 1 + step, 1, step).wait()
            sent(me, 3, step)
            arrive(elsewhere + dp + 1 + step, 3, step)


def gather_all(features, near, w_in, early, w_out, answers):
    n_dp, n_mp = lax.axis_size("dp"), lax.axis_size("mp")
    owners = answers.shape[0]
    items, in_part = features.shape
    dma = pltpu.SemaphoreType.DMA
    anywhere = pl.BlockSpec(memory_space=pl.ANY)
    return pl.pallas_call(
        gather_kernel,
        out_shape=(
            jax.ShapeDtypeStruct((items, n_mp * in_part), BF16),
            jax.ShapeDtypeStruct((owners, *w_in.shape), BF16),
            jax.ShapeDtypeStruct((owners, *w_out.shape), BF16),
            jax.ShapeDtypeStruct(answers.shape, BF16),
        ),
        in_specs=[anywhere] * 10,
        out_specs=[anywhere] * 4,
        scratch_shapes=[
            dma((6,)), dma((2, 2)), dma((2,)), dma((2,)),
            dma((2, n_dp, 2)), dma((2, n_dp, 2)), dma((2, n_dp, 2)), dma((2, n_dp, 2)),
            dma((owners,)), dma((owners,)),
        ],
        compiler_params=pltpu.CompilerParams(collective_id=0, has_side_effects=True),
    )(features, *near, w_in, *early, w_out, answers)


def shards(features, w_in, w_out, codebook, codes, decoder_grad):
    n_sec, n_dp, n_mp = (lax.axis_size(a) for a in ("section", "dp", "mp"))
    sec, dp, mp = (lax.axis_index(a) for a in ("section", "dp", "mp"))
    owners = n_sec * n_dp
    me = sec * n_dp + dp
    items, in_part = features.shape
    in_rows, hid = w_in.shape
    out_rows = w_out.shape[0]
    levels, rows_own, width = codebook.shape
    capacity = max(2, 2 * items // owners)
    slots = owners * capacity
    items_all = items * owners

    rightward = [(k, k + 1) for k in range(n_dp - 1)]
    leftward = [(k + 1, k) for k in range(n_dp - 1)]
    near = (shift(features, "mp", 1), shift(features, "mp", 2))
    right_1 = lax.ppermute(w_in, "dp", rightward)
    left_1 = lax.ppermute(w_in, "dp", leftward)

    exchange = functools.partial(
        lax.all_to_all, axis_name=("section", "dp"), split_axis=0, concat_axis=0, tiled=True
    )
    all_codes = exchange(jnp.broadcast_to(codes[None], (owners, levels, items)))
    mine = all_codes // rows_own == me
    before = jnp.arange(items)[:, None] < jnp.arange(items)[None, :]
    place = jnp.dot(
        mine.reshape(-1, items).astype(BF16), before.astype(BF16), preferred_element_type=F32
    ).astype(jnp.int32).reshape(owners, levels, items)
    place = jnp.where(mine, place, capacity)
    local = all_codes % rows_own
    hit = place[:, :, None, :] == jnp.arange(capacity)[None, None, :, None]
    asked = jnp.sum(jnp.where(hit, local[:, :, None, :], 0), axis=3)
    book = codebook.reshape(levels * rows_own, width)
    flat_asked = asked + (jnp.arange(levels) * rows_own)[None, :, None]
    flat_asked, right_1, left_1 = lax.optimization_barrier((flat_asked, right_1, left_1))
    right_2 = lax.ppermute(right_1, "dp", rightward)
    left_2 = lax.ppermute(left_1, "dp", leftward)
    f_full, w_full, out_full, answers = gather_all(
        features,
        near,
        w_in,
        (right_1, right_2, left_1, left_2),
        w_out,
        jnp.take(book, flat_asked, axis=0, mode="clip"),
    )
    w_full = w_full.reshape(owners * in_rows, hid)
    out_full = out_full.reshape(owners * out_rows, hid)
    owner_of = codes // rows_own
    same = (owner_of[:, :, None] == owner_of[:, None, :]) & before.T[None]
    ranking = jnp.sum(same.astype(jnp.int32), axis=2)
    level_ids = jnp.arange(levels, dtype=jnp.int32)[:, None]
    codewords = jnp.take(
        answers.reshape(owners * levels * capacity, width),
        (owner_of * levels + level_ids) * capacity + ranking,
        axis=0,
        mode="clip",
    )

    preact = jnp.dot(f_full, w_full, preferred_element_type=F32)
    hidden = jax.nn.silu(preact).astype(BF16)
    latent = None
    for step in list(range(1, n_mp)) + [0]:
        goes_to = target_of(mp, n_mp, step)
        rows = lax.dynamic_slice(out_full, (goes_to * width, 0), (width, hid))
        part = lax.dot_general(hidden, rows, (((1,), (1,)), ((), ())), preferred_element_type=F32)
        part = shift(part, "mp", step) if step else part
        latent = part if latent is None else latent + part

    residual = latent
    pull_sum = jnp.zeros_like(latent)
    inputs = []
    for level in range(levels):
        inputs.append(residual.astype(BF16))
        residual = residual - codewords[level].astype(F32)
        pull_sum = pull_sum + residual
    latent_grad = (
        (decoder_grad.astype(F32) + 2.0 * BETA * pull_sum) / jnp.sqrt(F32(items_all))
    ).astype(BF16)

    grad_full = jnp.zeros((items, n_mp * width), BF16)
    for step in range(n_mp):
        got = shift(latent_grad, "mp", step) if step else latent_grad
        at = source_of(mp, n_mp, step) if step else mp
        grad_full = lax.dynamic_update_slice(grad_full, got, (0, at * width))

    slot_of = owner_of * capacity + ranking
    pick = (jnp.arange(slots)[None, :, None] == slot_of[:, None, :]).astype(BF16)
    outgoing = lax.dot_general(
        pick, jnp.stack(inputs), (((2,), (1,)), ((0,), (0,))), preferred_element_type=F32
    ).astype(BF16)
    outgoing = outgoing.reshape(levels, owners, capacity, width).transpose(1, 0, 2, 3)
    incoming = exchange(outgoing)
    code_sums = sum_rows(
        asked.transpose(1, 0, 2).reshape(levels, slots),
        incoming.transpose(1, 0, 2, 3).reshape(levels, slots, width),
        rows_own,
    )

    back_hidden = jnp.dot(grad_full, out_full, preferred_element_type=F32)
    logistic = jax.nn.sigmoid(preact)
    slope = logistic * (1.0 + preact * (1.0 - logistic))
    pre_grad = (back_hidden * slope).astype(BF16)
    over_items = functools.partial(
        lax.dot_general, dimension_numbers=(((0,), (0,)), ((), ())), preferred_element_type=F32
    )

    def in_chunk(at):
        return over_items(lax.dynamic_slice(f_full, (0, at * in_rows), (items, in_rows)), pre_grad)

    def out_chunk(at):
        return over_items(lax.dynamic_slice(grad_full, (0, at * out_rows), (items, out_rows)), hidden)

    def scattered(chunk, sums):
        parts = []
        for step in list(range(n_dp - 1, 0, -1)) + [0]:
            goes_to = target_of(dp, n_dp, step) if step else dp
            pair = None
            for other in list(range(1, n_sec)) + [0]:
                to_sec = target_of(sec, n_sec, other) if other else sec
                part = chunk(to_sec * n_dp + goes_to)
                if other:
                    part = shift(part.astype(BF16), "section", other).astype(F32)
                pair = part if pair is None else pair + part
            if step:
                pair = shift(pair.astype(BF16), "dp", step).astype(F32)
            elif sums is not None:
                pair, sums = lax.optimization_barrier((pair, sums))
            parts.append(pair)
        total = parts[-1]
        for pair in parts[:-1]:
            total = total + pair
        return total, sums

    grads, code_sums = scattered(
        lambda at: jnp.concatenate([in_chunk(at), out_chunk(at)], axis=0), code_sums
    )
    in_grad, out_grad = grads[:in_rows], grads[in_rows:]
    return (in_grad, out_grad, code_sums)


def solution(mesh):
    owned = P(("section", "dp"), "mp")
    book = P(None, ("section", "dp"), "mp")
    return jax.shard_map(
        shards,
        mesh=mesh,
        in_specs=(owned, owned, owned, book, P(None, ("section", "dp")), owned),
        out_specs=(owned, owned, book),
        check_vma=False,
    )
```

```python
import functools

import jax
import jax.numpy as jnp
from jax import lax
from jax.experimental import pallas as pl
from jax.experimental.pallas import tpu as pltpu
from jax.sharding import PartitionSpec as P

BETA = 0.25
F32 = jnp.float32
BF16 = jnp.bfloat16


def partner_pairs(size, step):
    if size & (size - 1) == 0:
        return [(k, k ^ step) for k in range(size)]
    return [(k, (k + step) % size) for k in range(size)]


def source_of(me, size, step):
    if size & (size - 1) == 0:
        return me ^ step
    return (me + size - step) % size


def target_of(me, size, step):
    if size & (size - 1) == 0:
        return me ^ step
    return (me + step) % size


def shift(value, axis, step):
    return lax.ppermute(value, axis, partner_pairs(lax.axis_size(axis), step))


def sums_kernel(rows_ref, values_ref, out_ref):
    tile = out_ref.shape[1]
    slots = rows_ref.shape[2]
    first = pl.program_id(1) * tile
    row_ids = first + lax.broadcasted_iota(jnp.int32, (tile, slots), 0)
    chosen = jnp.where(row_ids == rows_ref[0], 1.0, 0.0).astype(BF16)
    out_ref[0] = jnp.dot(chosen, values_ref[0], preferred_element_type=F32)


def sum_rows(rows, values, rows_own):
    levels, slots = rows.shape
    width = values.shape[2]
    tile = min(512, rows_own)
    return pl.pallas_call(
        sums_kernel,
        grid=(levels, rows_own // tile),
        in_specs=[
            pl.BlockSpec((1, 1, slots), lambda level, part: (level, 0, 0)),
            pl.BlockSpec((1, slots, width), lambda level, part: (level, 0, 0)),
        ],
        out_specs=pl.BlockSpec((1, tile, width), lambda level, part: (level, part, 0)),
        out_shape=jax.ShapeDtypeStruct((levels, rows_own, width), F32),
        compiler_params=pltpu.CompilerParams(vmem_limit_bytes=24 * 2**20),
        cost_estimate=pl.CostEstimate(
            flops=2 * levels * rows_own * slots * width,
            bytes_accessed=4 * levels * rows_own * width,
            transcendentals=0,
        ),
    )(rows.reshape(levels, 1, slots), values)


def gather_kernel(
    f_ref, fx_ref, fy_ref, w_ref, r1_ref, r2_ref, l1_ref, l2_ref, o_ref, ans_ref,
    f_out, w_out, o_out, ans_out, local_sem, early_sem, f_send, f_recv, dp_send, dp_recv, sec_send, sec_recv, ans_send, ans_recv,
):
    n_dp, n_mp = lax.axis_size("dp"), lax.axis_size("mp")
    sec, dp, mp = (lax.axis_index(a) for a in ("section", "dp", "mp"))
    owners = ans_ref.shape[0]
    me = sec * n_dp + dp
    base = sec * n_dp
    other = {"section": 1 - sec}
    items, in_part = f_ref.shape
    barrier = pltpu.get_barrier_semaphore()

    def owner_at(step):
        at = lax.rem(me + step, owners)
        return at, {"section": at // n_dp, "dp": lax.rem(at, n_dp)}

    for step in range(1, owners):
        pl.semaphore_signal(barrier, inc=1, device_id=owner_at(step)[1], device_id_type=pl.DeviceIdType.MESH)
    for step in range(1, n_mp):
        pl.semaphore_signal(
            barrier, inc=1, device_id={"mp": target_of(mp, n_mp, step)}, device_id_type=pl.DeviceIdType.MESH
        )
    pl.semaphore_wait(barrier, owners - 1 + n_mp - 1)

    def remote(src, dst, send, recv, to):
        return pltpu.make_async_remote_copy(
            src_ref=src, dst_ref=dst, send_sem=send, recv_sem=recv,
            device_id=to, device_id_type=pl.DeviceIdType.MESH,
        )

    def columns(at):
        return pl.ds(pl.multiple_of(at * in_part, in_part), in_part)

    answers = []
    for step in range(1, owners):
        at, to = owner_at(step)
        answers.append(remote(ans_ref.at[at], ans_out.at[me], ans_send.at[step], ans_recv.at[step], to))
        answers[-1].start()

    half = items // 2
    early = ((r1_ref, r2_ref), (l1_ref, l2_ref))
    halves = []
    for k, (ref, to) in enumerate(((fx_ref, mp ^ 2), (fy_ref, mp ^ 1))):
        rows = pl.ds(k * half, half)
        halves.append(
            remote(
                ref.at[rows], f_out.at[rows, columns(to ^ 3)], f_send.at[k], f_recv.at[k], {"mp": to}
            )
        )

    def weights(block, src, side, step, to):
        along = side < 2
        place = side if along else side - 2
        sems = (dp_send, dp_recv) if along else (sec_send, sec_recv)
        came = step - 1 if along else step
        copies = []
        for k, (own, out) in enumerate(((w_ref, w_out), (o_ref, o_out))):
            if k == 0 and along and step < 2:
                continue
            held = early[place][came] if k == 0 and 0 <= came < 2 else out.at[block]
            copies.append(
                remote(
                    own if src is None else held, out.at[block],
                    sems[0].at[place, step, k], sems[1].at[place, step, k], to,
                )
            )
        return copies

    def early_copy(block, side, step):
        return pltpu.make_async_copy(early[side][step], w_out.at[block], early_sem.at[side, step])

    def start(copies):
        for copy in copies:
            copy.start()

    right, left = {"dp": dp + 1}, {"dp": dp - 1}

    @pl.when(dp < n_dp - 1)
    def _():
        start(weights(me, None, 0, 0, right))

    @pl.when(dp > 0)
    def _():
        start(weights(me, None, 1, 0, left))

    start(halves)
    own_sec = weights(me, None, 2, n_dp - 1, other)
    start(own_sec)
    locals_ = [
        pltpu.make_async_copy(f_ref, f_out.at[:, columns(mp)], local_sem.at[0]),
        pltpu.make_async_copy(fx_ref, f_out.at[:, columns(mp ^ 1)], local_sem.at[4]),
        pltpu.make_async_copy(fy_ref, f_out.at[:, columns(mp ^ 2)], local_sem.at[5]),
        pltpu.make_async_copy(w_ref, w_out.at[me], local_sem.at[1]),
        pltpu.make_async_copy(o_ref, o_out.at[me], local_sem.at[2]),
        pltpu.make_async_copy(ans_ref.at[me], ans_out.at[me], local_sem.at[3]),
    ]
    start(locals_)

    def arrive(block, side, step):
        for copy in weights(block, block, side, step, other):
            copy.wait_recv()

    for step in range(n_dp - 1):
        @pl.when(dp - 1 - step >= 0)
        def _(step=step):
            block = base + dp - 1 - step
            if step < 2:
                early_copy(block, 0, step).start()
            arrive(block, 0, step)
            if step + 1 < n_dp - 1:
                @pl.when(dp < n_dp - 1)
                def _():
                    start(weights(block, block, 0, step + 1, right))
            start(weights(block, block, 2, step, other))

        @pl.when(dp + 1 + step <= n_dp - 1)
        def _(step=step):
            block = base + dp + 1 + step
            if step < 2:
                early_copy(block, 1, step).start()
            arrive(block, 1, step)
            if step + 1 < n_dp - 1:
                @pl.when(dp > 0)
                def _():
                    start(weights(block, block, 1, step + 1, left))
            start(weights(block, block, 3, step, other))

    for copy in locals_ + answers:
        copy.wait()
    for copy in halves:
        copy.wait_send()
    for k in range(2):
        view = f_out.at[pl.ds(k * half, half), columns(mp ^ 3)]
        remote(view, view, f_send.at[k], f_recv.at[k], {"mp": mp ^ 1}).wait_recv()
    elsewhere = (1 - sec) * n_dp
    for copy in own_sec:
        copy.wait_send()
    arrive(elsewhere + dp, 2, n_dp - 1)

    def sent(block, side, step):
        for copy in weights(block, block, side, step, other):
            copy.wait_send()

    @pl.when(dp < n_dp - 1)
    def _():
        sent(me, 0, 0)

    @pl.when(dp > 0)
    def _():
        sent(me, 1, 0)

    for step in range(n_dp - 1):
        @pl.when(dp - 1 - step >= 0)
        def _(step=step):
            if step + 1 < n_dp - 1:
                @pl.when(dp < n_dp - 1)
                def _():
                    sent(me, 0, step + 1)
            if step < 2:
                early_copy(base + dp - 1 - step, 0, step).wait()
            sent(me, 2, step)
            arrive(elsewhere + dp - 1 - step, 2, step)

        @pl.when(dp + 1 + step <= n_dp - 1)
        def _(step=step):
            if step + 1 < n_dp - 1:
                @pl.when(dp > 0)
                def _():
                    sent(me, 1, step + 1)
            if step < 2:
                early_copy(base + dp + 1 + step, 1, step).wait()
            sent(me, 3, step)
            arrive(elsewhere + dp + 1 + step, 3, step)


def gather_all(features, near, w_in, early, w_out, answers):
    n_dp, n_mp = lax.axis_size("dp"), lax.axis_size("mp")
    owners = answers.shape[0]
    items, in_part = features.shape
    dma = pltpu.SemaphoreType.DMA
    anywhere = pl.BlockSpec(memory_space=pl.ANY)
    return pl.pallas_call(
        gather_kernel,
        out_shape=(
            jax.ShapeDtypeStruct((items, n_mp * in_part), BF16),
            jax.ShapeDtypeStruct((owners, *w_in.shape), BF16),
            jax.ShapeDtypeStruct((owners, *w_out.shape), BF16),
            jax.ShapeDtypeStruct(answers.shape, BF16),
        ),
        in_specs=[pl.BlockSpec(memory_space=pltpu.VMEM)] * 10,
        out_specs=[anywhere] * 4,
        scratch_shapes=[
            dma((6,)), dma((2, 2)), dma((2,)), dma((2,)),
            dma((2, n_dp, 2)), dma((2, n_dp, 2)), dma((2, n_dp, 2)), dma((2, n_dp, 2)),
            dma((owners,)), dma((owners,)),
        ],
        compiler_params=pltpu.CompilerParams(
            collective_id=0, has_side_effects=True, vmem_limit_bytes=24 * 2**20
        ),
    )(features, *near, w_in, *early, w_out, answers)


def shards(features, w_in, w_out, codebook, codes, decoder_grad):
    n_sec, n_dp, n_mp = (lax.axis_size(a) for a in ("section", "dp", "mp"))
    sec, dp, mp = (lax.axis_index(a) for a in ("section", "dp", "mp"))
    owners = n_sec * n_dp
    me = sec * n_dp + dp
    items, in_part = features.shape
    in_rows, hid = w_in.shape
    out_rows = w_out.shape[0]
    levels, rows_own, width = codebook.shape
    capacity = max(2, 2 * items // owners)
    slots = owners * capacity
    items_all = items * owners

    rightward = [(k, k + 1) for k in range(n_dp - 1)]
    leftward = [(k + 1, k) for k in range(n_dp - 1)]
    near = (shift(features, "mp", 1), shift(features, "mp", 2))
    right_1 = lax.ppermute(w_in, "dp", rightward)
    left_1 = lax.ppermute(w_in, "dp", leftward)

    exchange = functools.partial(
        lax.all_to_all, axis_name=("section", "dp"), split_axis=0, concat_axis=0, tiled=True
    )
    all_codes = exchange(jnp.broadcast_to(codes[None], (owners, levels, items)))
    mine = all_codes // rows_own == me
    before = jnp.arange(items)[:, None] < jnp.arange(items)[None, :]
    place = jnp.dot(
        mine.reshape(-1, items).astype(BF16), before.astype(BF16), preferred_element_type=F32
    ).astype(jnp.int32).reshape(owners, levels, items)
    place = jnp.where(mine, place, capacity)
    local = all_codes % rows_own
    hit = place[:, :, None, :] == jnp.arange(capacity)[None, None, :, None]
    asked = jnp.sum(jnp.where(hit, local[:, :, None, :], 0), axis=3)
    book = codebook.reshape(levels * rows_own, width)
    flat_asked = asked + (jnp.arange(levels) * rows_own)[None, :, None]
    flat_asked, right_1, left_1 = lax.optimization_barrier((flat_asked, right_1, left_1))
    right_2 = lax.ppermute(right_1, "dp", rightward)
    left_2 = lax.ppermute(left_1, "dp", leftward)
    f_full, w_full, out_full, answers = gather_all(
        features,
        near,
        w_in,
        (right_1, right_2, left_1, left_2),
        w_out,
        jnp.take(book, flat_asked, axis=0, mode="clip"),
    )
    w_full = w_full.reshape(owners * in_rows, hid)
    out_full = out_full.reshape(owners * out_rows, hid)
    owner_of = codes // rows_own
    same = (owner_of[:, :, None] == owner_of[:, None, :]) & before.T[None]
    ranking = jnp.sum(same.astype(jnp.int32), axis=2)
    level_ids = jnp.arange(levels, dtype=jnp.int32)[:, None]
    codewords = jnp.take(
        answers.reshape(owners * levels * capacity, width),
        (owner_of * levels + level_ids) * capacity + ranking,
        axis=0,
        mode="clip",
    )

    preact = jnp.dot(f_full, w_full, preferred_element_type=F32)
    hidden = jax.nn.silu(preact).astype(BF16)
    latent = None
    for step in list(range(1, n_mp)) + [0]:
        goes_to = target_of(mp, n_mp, step)
        rows = lax.dynamic_slice(out_full, (goes_to * width, 0), (width, hid))
        part = lax.dot_general(hidden, rows, (((1,), (1,)), ((), ())), preferred_element_type=F32)
        part = shift(part, "mp", step) if step else part
        latent = part if latent is None else latent + part

    residual = latent
    pull_sum = jnp.zeros_like(latent)
    inputs = []
    for level in range(levels):
        inputs.append(residual.astype(BF16))
        residual = residual - codewords[level].astype(F32)
        pull_sum = pull_sum + residual
    latent_grad = (
        (decoder_grad.astype(F32) + 2.0 * BETA * pull_sum) / jnp.sqrt(F32(items_all))
    ).astype(BF16)

    grad_full = jnp.zeros((items, n_mp * width), BF16)
    for step in range(n_mp):
        got = shift(latent_grad, "mp", step) if step else latent_grad
        at = source_of(mp, n_mp, step) if step else mp
        grad_full = lax.dynamic_update_slice(grad_full, got, (0, at * width))

    slot_of = owner_of * capacity + ranking
    pick = (jnp.arange(slots)[None, :, None] == slot_of[:, None, :]).astype(BF16)
    outgoing = lax.dot_general(
        pick, jnp.stack(inputs), (((2,), (1,)), ((0,), (0,))), preferred_element_type=F32
    ).astype(BF16)
    outgoing = outgoing.reshape(levels, owners, capacity, width).transpose(1, 0, 2, 3)
    incoming = exchange(outgoing)
    code_sums = sum_rows(
        asked.transpose(1, 0, 2).reshape(levels, slots),
        incoming.transpose(1, 0, 2, 3).reshape(levels, slots, width),
        rows_own,
    )

    back_hidden = jnp.dot(grad_full, out_full, preferred_element_type=F32)
    logistic = jax.nn.sigmoid(preact)
    slope = logistic * (1.0 + preact * (1.0 - logistic))
    pre_grad = (back_hidden * slope).astype(BF16)
    over_items = functools.partial(
        lax.dot_general, dimension_numbers=(((0,), (0,)), ((), ())), preferred_element_type=F32
    )

    def in_chunk(at):
        return over_items(lax.dynamic_slice(f_full, (0, at * in_rows), (items, in_rows)), pre_grad)

    def out_chunk(at):
        return over_items(lax.dynamic_slice(grad_full, (0, at * out_rows), (items, out_rows)), hidden)

    def scattered(chunk, sums):
        parts = []
        for step in list(range(n_dp - 1, 0, -1)) + [0]:
            goes_to = target_of(dp, n_dp, step) if step else dp
            pair = None
            for other in list(range(1, n_sec)) + [0]:
                to_sec = target_of(sec, n_sec, other) if other else sec
                part = chunk(to_sec * n_dp + goes_to)
                if other:
                    part = shift(part.astype(BF16), "section", other).astype(F32)
                pair = part if pair is None else pair + part
            if step:
                pair = shift(pair.astype(BF16), "dp", step).astype(F32)
            elif sums is not None:
                pair, sums = lax.optimization_barrier((pair, sums))
            parts.append(pair)
        total = parts[-1]
        for pair in parts[:-1]:
            total = total + pair
        return total, sums

    grads, code_sums = scattered(
        lambda at: jnp.concatenate([in_chunk(at), out_chunk(at)], axis=0), code_sums
    )
    in_grad, out_grad = grads[:in_rows], grads[in_rows:]
    return (in_grad, out_grad, code_sums)


def solution(mesh):
    owned = P(("section", "dp"), "mp")
    book = P(None, ("section", "dp"), "mp")
    return jax.shard_map(
        shards,
        mesh=mesh,
        in_specs=(owned, owned, owned, book, P(None, ("section", "dp")), owned),
        out_specs=(owned, owned, book),
        check_vma=False,
    )
```
